128 devices in a mesh: grp: 2 (over core), dev: 64 (over x, y, z).
Axes of the slice: x: 4, y: 4, z: 4, core: 2. Of those that a mesh axis runs over, the one named last changes fastest.
Arguments:
- states: bfloat16 [2048, 3584], P(('grp', 'dev')), may hold values from -6 to 6
- routes: int32 [2048, 8], P(('grp', 'dev')), may hold values from 0 to 127, all different within a row; in each aligned block of 16 rows (0 to 15, 16 to 31, ...) at most 2 rows name the same one
- gate_scores: float32 [2048, 8], P(('grp', 'dev')), may hold values from 0.05 to 1
- w_in: bfloat16 [128, 3584, 2048], P(('grp', 'dev')), may hold values from -0.09375 to 0.09375
- w_out: bfloat16 [128, 1024, 3584], P(('grp', 'dev')), may hold values from -0.1875 to 0.1875
Outputs:
- mixed: bfloat16 [2048, 3584], P(('grp', 'dev'))
The draws below stay inside these ranges and needn't reach their ends.
Inputs may be any that keep to these rules, and one draw needn't show every extreme that they name: `routes`: each row names 8 different experts; among the rows of one device no expert is named by more than 2 rows, a bound that some block reaches of some device in every draw.
All inputs are finite; a program needn't handle non-finite values.
Results may differ from the reference program's by a relative error of at most 0.0051.
Values may be sent and summed in bfloat16 or wider, within the bound.
No kernel may reach another device: no remote copies, remote signals or barrier semaphores. Data moves between devices by JAX's collectives and lax.ppermute only.
A program may use at most 64 MiB of HBM per device.

```python
import math
import jax
import jax.numpy as jnp
import numpy as np
from jax import lax

D = 3584
HID = 1024
TOP = 8
ROW_DEV = 16
EXPERTS = 128
ROWS = 2048
MOST = 2


def level_of(rng, shape, cuts, smallest, largest):
    loudness, own = 1.0, jax.random.fold_in(rng, 6)
    for axis_at, shards_of in cuts:
        steps = jnp.exp(jax.random.uniform(jax.random.fold_in(own, axis_at), (shards_of,), jnp.float32, smallest / len(cuts), largest / len(cuts)))
        loudness = loudness * jnp.repeat(steps, shape[axis_at] // shards_of).reshape([-1 if axis == axis_at else 1 for axis in range(len(shape))])
    return loudness


def shared_out(own_key, own, number, rows, count, top, reach, lean):
    sequence = jax.random.permutation(own_key, count)
    packed, usual = portions_of(count, rows * top, reach, lean, True), portions_of(count, rows * top, reach, lean, False)
    places = jnp.arange(count)

    def named(tallies, turn):
        used = int((tallies > 0).sum())
        fixed = max(1, used // 4)
        moved = fixed + (places - fixed + turn * (used - fixed)) % max(1, count - fixed)
        return jnp.zeros((count,), jnp.int32).at[sequence[jnp.where(places < fixed, places, moved)]].set(jnp.asarray(tallies, jnp.int32))

    tallies = jnp.where(number % 4 == 0, named(packed, number // 4), named(usual, number - number // 4 - 1))
    mixed = jax.random.permutation(jax.random.fold_in(own, 3), count)
    source_of, sink = mixed[0:count // 2 * 2:2], mixed[1:count // 2 * 2:2]
    margin = jnp.minimum(tallies[source_of] - 1, reach - tallies[sink]) // 2
    margin = jnp.where((source_of == sequence[0]) | (sink == sequence[0]) | (tallies[sink] == 0), 0, jnp.maximum(margin, 0))
    moved = jax.random.randint(jax.random.fold_in(own, 4), (count // 2,), 0, 1 << 20) % (margin + 1)
    tallies = tallies.at[source_of].add(-moved).at[sink].add(moved)
    labels = jnp.searchsorted(jnp.cumsum(tallies), jnp.arange(rows * top), side="right").astype(jnp.int32)
    grid = labels.reshape(top, rows).T
    grid = grid[jax.random.permutation(jax.random.fold_in(own, 1), rows)]
    turn = jax.random.randint(jax.random.fold_in(own, 2), (rows, 1), 0, top)
    return jnp.take_along_axis(grid, (jnp.arange(top)[None, :] + turn) % top, axis=1)


def portions_of(amount, total, most, skew, full):
    loads = [(1 << 20) // math.isqrt(grade ** skew) + 1 for grade in range(1, amount + 1)]
    largest = most if full else min(most, max(-(-total // amount), total * loads[0] // sum(loads)))
    least = 1 if total - largest >= amount - 1 else 0
    given, rest = [largest] + [least] * (amount - 1), total - largest - least * (amount - 1)
    while rest > 0:
        free = [i for i in range(1, amount) if given[i] < largest] or [i for i in range(1, amount) if given[i] < most]
        pool, remaining = sum([loads[i] for i in free]), rest
        for i in free:
            addition = min(most - given[i], max(1, remaining * loads[i] // pool), rest)
            given[i] = given[i] + addition
            rest = rest - addition
    return np.array(given)


def scatter_about(key, extent, spread, most, pieces=(), kind=jnp.bfloat16):
    values = spread * jax.random.normal(key, extent, jnp.float32)
    if pieces:
        values = values * level_of(key, extent, pieces, -0.22, 0.18)
    return jnp.clip(values, -most, most).astype(kind)


def setup_inputs(seed: int = 0) -> dict:
    key_of = jax.random.split(jax.random.key(seed), 6)
    states = scatter_about(key_of[0], (ROWS, D), 1.0, 6.0, ((0, 128),))
    routes_keys = jax.random.split(jax.random.fold_in(key_of[1], 1), ROWS // ROW_DEV)
    routes_turns = jax.random.permutation(jax.random.fold_in(key_of[1], 3), ROWS // ROW_DEV)
    routes = jax.vmap(lambda own, number: shared_out(jax.random.fold_in(key_of[1], 2), own, number, ROW_DEV, EXPERTS, TOP, MOST, 2))(routes_keys, routes_turns).reshape((ROWS, TOP))
    gate_scores = jnp.clip(jnp.exp(math.log(1.0) - 2.9957323 * jax.random.uniform(key_of[2], (ROWS, TOP), jnp.float32) ** level_of(key_of[2], (ROWS, TOP), ((0, 128),), -0.2, 0.2)), 0.05, 1.0)
    w_in = scatter_about(key_of[3], (EXPERTS, D, 2 * HID), D ** -0.5, 0.09375, ((0, 128),))
    w_out = scatter_about(key_of[4], (EXPERTS, HID, D), HID ** -0.5, 0.1875, ((0, 128),))
    return {"states": states, "routes": routes, "gate_scores": gate_scores, "w_in": w_in, "w_out": w_out}


route_scale = 2.5


def expert_ffn(inputs, w_first, w_second):
    projected = jnp.dot(inputs, w_first, preferred_element_type=jnp.float32)
    width = w_second.shape[0]
    gate_part = projected[:, :width]
    up_part = projected[:, width:]
    hidden = (jax.nn.silu(gate_part) * up_part).astype(jnp.bfloat16)
    return jnp.dot(hidden, w_second, preferred_element_type=jnp.float32).astype(jnp.bfloat16)


def reference(states, routes, gate_scores, w_in, w_out):
    blocks = ROWS // ROW_DEV
    count = ROW_DEV * TOP
    chosen = routes.reshape(blocks, count).astype(jnp.int32)
    onehot = (chosen[:, :, None] == jnp.arange(EXPERTS, dtype=jnp.int32)[None, None, :]).astype(jnp.int32)
    position = jnp.sum(jnp.cumsum(onehot, axis=1) * onehot, axis=2) - 1
    source = jnp.broadcast_to(jnp.arange(blocks, dtype=jnp.int32)[:, None], (blocks, count))
    row_ids = source * ROW_DEV + jnp.broadcast_to((jnp.arange(count, dtype=jnp.int32) // TOP)[None, :], (blocks, count))
    weights = gate_scores / jnp.sum(gate_scores, axis=1, keepdims=True) * route_scale
    weights = weights.reshape(blocks, count)
    indices = jnp.full((EXPERTS, blocks, MOST), ROWS, jnp.int32).at[chosen, source, position].set(row_ids)
    scales = jnp.zeros((EXPERTS, blocks, MOST), jnp.float32).at[chosen, source, position].set(weights)
    padded = jnp.concatenate([states, jnp.zeros((1, D), states.dtype)], axis=0)

    def expert_step(totals, entries):
        index_row, scale_row, w_first, w_second = entries
        flat_index = index_row.reshape(-1)
        result = expert_ffn(padded[flat_index], w_first, w_second)
        totals = totals.at[flat_index].add(scale_row.reshape(-1)[:, None] * result.astype(jnp.float32))
        return totals, None

    totals, _ = lax.scan(expert_step, jnp.zeros((ROWS + 1, D), jnp.float32), (indices, scales, w_in, w_out))
    return (states.astype(jnp.float32) + totals[:ROWS]).astype(jnp.bfloat16)
```

```python
import functools

import jax
import jax.numpy as jnp
from jax import lax
from jax.experimental import pallas as pl
from jax.experimental.pallas import tpu as pltpu
from jax.sharding import PartitionSpec as P

route_scale = 2.5
axes = ("grp", "dev")
most = 2
parts = 4
lines = most * parts
group = 16


def slot_of(routes, columns):
    rows, top = routes.shape
    column = lax.broadcasted_iota(jnp.int32, (rows, columns), 1)
    expert = column // lines
    named = jnp.zeros((rows, columns), jnp.float32)
    for k in range(top):
        named = named + (routes[:, k : k + 1] == expert).astype(jnp.float32)
    earlier = (
        lax.broadcasted_iota(jnp.int32, (rows, rows), 0)
        > lax.broadcasted_iota(jnp.int32, (rows, rows), 1)
    ).astype(jnp.float32)
    position = jnp.dot(earlier, named, preferred_element_type=jnp.float32)
    slot = (column % most).astype(jnp.float32)
    return expert, (named > 0.5) & (jnp.abs(position - slot) < 0.5), column // most % parts


def dispatch_kernel(routes_ref, states_ref, out_ref):
    rows, width = states_ref.shape
    columns, piece = out_ref.shape
    _, filled, part = slot_of(routes_ref[...], columns)
    pick = jnp.concatenate(
        [(filled & (part == p)).astype(jnp.float32) for p in range(parts)], axis=0
    ).astype(jnp.bfloat16)
    source = jnp.concatenate(
        [states_ref[:, p * piece : (p + 1) * piece] for p in range(parts)], axis=0
    )
    step = 128
    for c in range(0, columns, step):
        block = lax.dot_general(
            pick[:, c : c + step],
            source,
            (((0,), (0,)), ((), ())),
            preferred_element_type=jnp.float32,
        )
        out_ref[c : c + step, :] = block.astype(jnp.bfloat16)


def combine_kernel(routes_ref, scores_ref, states_ref, got_ref, out_ref):
    rows, width = states_ref.shape
    columns, piece = got_ref.shape
    routes = routes_ref[...]
    scores = scores_ref[...]
    weights = scores / jnp.sum(scores, axis=1, keepdims=True) * route_scale
    expert, filled, part = slot_of(routes, columns)
    weight = jnp.zeros((rows, columns), jnp.float32)
    for k in range(routes.shape[1]):
        weight = weight + jnp.where(routes[:, k : k + 1] == expert, weights[:, k : k + 1], 0.0)
    weight = jnp.where(filled, weight, 0.0)
    high = weight.astype(jnp.bfloat16).astype(jnp.float32)
    low = weight - high
    mix = jnp.concatenate(
        [jnp.where(part == p, w, 0.0) for w in (high, low) for p in range(parts)], axis=0
    ).astype(jnp.bfloat16)
    total = jnp.dot(mix, got_ref[...], preferred_element_type=jnp.float32)
    for p in range(parts):
        both = total[p * rows : (p + 1) * rows] + total[(parts + p) * rows : (parts + p + 1) * rows]
        own = states_ref[:, p * piece : (p + 1) * piece].astype(jnp.float32)
        out_ref[:, p * piece : (p + 1) * piece] = (own + both).astype(jnp.bfloat16)


def regroup(inverse):
    size = group * lines
    there = lax.broadcasted_iota(jnp.int32, (size, size), 1 if inverse else 0)
    here = lax.broadcasted_iota(jnp.int32, (size, size), 0 if inverse else 1)
    part = there // (group * most)
    message = there % (group * most) // most
    match = here == message * lines + part * most + there % most
    return match.astype(jnp.float32).astype(jnp.bfloat16)


def ffn_kernel(
    in_ref, first_hbm, second_hbm, out_ref, first, second, rows_in, hidden, rows_out, first_sem, second_sem
):
    chunks, deep, both = first.shape
    half = both // 2
    _, piece = in_ref.shape
    slots = rows_in.shape[1]
    copies = []
    for c in range(chunks):
        for h in range(2):
            copies.append(
                pltpu.make_async_copy(
                    first_hbm.at[0, :, pl.ds(h * half * chunks + c * half, half)],
                    first.at[c, :, pl.ds(h * half, half)],
                    first_sem.at[c, h],
                )
            )
    for p in range(parts):
        copies.append(
            pltpu.make_async_copy(
                second_hbm.at[0, :, pl.ds(p * piece, piece)], second.at[p], second_sem.at[p]
            )
        )
    for copy in copies:
        copy.start()
    size = group * lines
    each = group * most
    order = regroup(False)
    for c in range(in_ref.shape[0] // size):
        block = jnp.dot(order, in_ref[c * size : (c + 1) * size, :], preferred_element_type=jnp.float32)
        block = block.astype(jnp.bfloat16)
        for p in range(parts):
            rows_in[p, c * each : (c + 1) * each, :] = block[p * each : (p + 1) * each]
    for c in range(chunks):
        copies[2 * c].wait()
        copies[2 * c + 1].wait()
        total = jnp.zeros((slots, both), jnp.float32)
        for p in range(parts):
            total = total + jnp.dot(
                rows_in[p], first[c, p * piece : (p + 1) * piece, :], preferred_element_type=jnp.float32
            )
        gate, up = total[:, :half], total[:, half:]
        hidden[:, c * half : (c + 1) * half] = (gate / (1.0 + jnp.exp(-gate)) * up).astype(jnp.bfloat16)
    for p in range(parts):
        copies[2 * chunks + p].wait()
        rows_out[p] = jnp.dot(hidden[...], second[p], preferred_element_type=jnp.float32).astype(
            jnp.bfloat16
        )
    back = regroup(True)
    for c in range(out_ref.shape[0] // size):
        block = jnp.concatenate([rows_out[p, c * each : (c + 1) * each, :] for p in range(parts)], axis=0)
        block = jnp.dot(back, block, preferred_element_type=jnp.float32)
        out_ref[c * size : (c + 1) * size, :] = block.astype(jnp.bfloat16)


def body(states, routes, gate_scores, w_in, w_out):
    rows, width = states.shape
    experts = lax.axis_size(axes)
    piece = width // parts
    columns = experts * lines
    slots = experts * most
    _, deep, both = w_in.shape
    inner = w_out.shape[1]
    chunks = 4
    vmem = pl.BlockSpec(memory_space=pltpu.VMEM)
    hbm = pl.BlockSpec(memory_space=pl.ANY)
    message = jax.ShapeDtypeStruct((columns, piece), jnp.bfloat16)

    outgoing = pl.pallas_call(
        dispatch_kernel,
        out_shape=message,
        in_specs=[vmem] * 2,
        out_specs=vmem,
        compiler_params=pltpu.CompilerParams(vmem_limit_bytes=24 << 20),
        name="dispatch",
    )(routes, states)
    received = lax.all_to_all(outgoing, axes, split_axis=0, concat_axis=0, tiled=True)
    result = pl.pallas_call(
        ffn_kernel,
        out_shape=message,
        in_specs=[vmem, hbm, hbm],
        out_specs=vmem,
        scratch_shapes=[
            pltpu.VMEM((chunks, deep, both // chunks), jnp.bfloat16),
            pltpu.VMEM((parts, inner, piece), jnp.bfloat16),
            pltpu.VMEM((parts, slots, piece), jnp.bfloat16),
            pltpu.VMEM((slots, inner), jnp.bfloat16),
            pltpu.VMEM((parts, slots, piece), jnp.bfloat16),
            pltpu.SemaphoreType.DMA((chunks, 2)),
            pltpu.SemaphoreType.DMA((parts,)),
        ],
        compiler_params=pltpu.CompilerParams(vmem_limit_bytes=48 << 20),
        cost_estimate=pl.CostEstimate(
            flops=2 * slots * width * inner * 3, bytes_accessed=2 * width * inner * 3, transcendentals=slots * inner
        ),
        name="expert_ffn",
    )(received, w_in, w_out)
    returned = lax.all_to_all(result, axes, split_axis=0, concat_axis=0, tiled=True)
    return pl.pallas_call(
        combine_kernel,
        out_shape=jax.ShapeDtypeStruct((rows, width), jnp.bfloat16),
        in_specs=[vmem] * 4,
        out_specs=vmem,
        compiler_params=pltpu.CompilerParams(vmem_limit_bytes=24 << 20),
        name="combine",
    )(routes, gate_scores, states, returned)


def solution(mesh):
    return jax.shard_map(
        body,
        mesh=mesh,
        in_specs=(
            P(axes, None),
            P(axes, None),
            P(axes, None),
            P(axes, None, None),
            P(axes, None, None),
        ),
        out_specs=P(axes, None),
        check_vma=False,
    )
```

```python
import functools

import jax
import jax.numpy as jnp
from jax import lax
from jax.experimental import pallas as pl
from jax.experimental.pallas import tpu as pltpu
from jax.sharding import PartitionSpec as P

route_scale = 2.5
axes = ("grp", "dev")
most = 2
parts = 4
lines = most * parts
group = 16


def slot_of(routes, columns):
    rows, top = routes.shape
    column = lax.broadcasted_iota(jnp.int32, (rows, columns), 1)
    expert = column // lines
    named = jnp.zeros((rows, columns), jnp.float32)
    for k in range(top):
        named = named + (routes[:, k : k + 1] == expert).astype(jnp.float32)
    earlier = (
        lax.broadcasted_iota(jnp.int32, (rows, rows), 0)
        > lax.broadcasted_iota(jnp.int32, (rows, rows), 1)
    ).astype(jnp.float32)
    position = jnp.dot(earlier, named, preferred_element_type=jnp.float32)
    slot = (column % most).astype(jnp.float32)
    return expert, (named > 0.5) & (jnp.abs(position - slot) < 0.5), column // most % parts


def dispatch_kernel(routes_ref, states_ref, out_ref):
    rows, width = states_ref.shape
    columns, piece = out_ref.shape
    _, filled, part = slot_of(routes_ref[...].T, columns)
    pick = jnp.concatenate(
        [(filled & (part == p)).astype(jnp.float32) for p in range(parts)], axis=0
    ).astype(jnp.bfloat16)
    source = jnp.concatenate(
        [states_ref[:, p * piece : (p + 1) * piece] for p in range(parts)], axis=0
    )
    step = 128
    for c in range(0, columns, step):
        block = lax.dot_general(
            pick[:, c : c + step],
            source,
            (((0,), (0,)), ((), ())),
            preferred_element_type=jnp.float32,
        )
        out_ref[c : c + step, :] = block.astype(jnp.bfloat16)


def combine_kernel(routes_ref, scores_ref, states_ref, got_ref, out_ref):
    rows, width = states_ref.shape
    columns, piece = got_ref.shape
    routes = routes_ref[...].T
    scores = scores_ref[...].T
    weights = scores / jnp.sum(scores, axis=1, keepdims=True) * route_scale
    expert, filled, part = slot_of(routes, columns)
    weight = jnp.zeros((rows, columns), jnp.float32)
    for k in range(routes.shape[1]):
        weight = weight + jnp.where(routes[:, k : k + 1] == expert, weights[:, k : k + 1], 0.0)
    weight = jnp.where(filled, weight, 0.0)
    high = weight.astype(jnp.bfloat16).astype(jnp.float32)
    low = weight - high
    mix = jnp.concatenate(
        [jnp.where(part == p, w, 0.0) for w in (high, low) for p in range(parts)], axis=0
    ).astype(jnp.bfloat16)
    total = jnp.dot(mix, got_ref[...], preferred_element_type=jnp.float32)
    for p in range(parts):
        both = total[p * rows : (p + 1) * rows] + total[(parts + p) * rows : (parts + p + 1) * rows]
        own = states_ref[:, p * piece : (p + 1) * piece].astype(jnp.float32)
        out_ref[:, p * piece : (p + 1) * piece] = (own + both).astype(jnp.bfloat16)


def regroup(inverse):
    size = group * lines
    there = lax.broadcasted_iota(jnp.int32, (size, size), 1 if inverse else 0)
    here = lax.broadcasted_iota(jnp.int32, (size, size), 0 if inverse else 1)
    part = there // (group * most)
    message = there % (group * most) // most
    match = here == message * lines + part * most + there % most
    return match.astype(jnp.float32).astype(jnp.bfloat16)


def ffn_kernel(in_ref, first, second, out_ref, rows_in, hidden, rows_out):
    _, deep, both = first.shape
    inner = both // 2
    _, piece = in_ref.shape
    slots = rows_in.shape[1]
    size = group * lines
    each = group * most
    order = regroup(False)
    for c in range(in_ref.shape[0] // size):
        block = jnp.dot(order, in_ref[c * size : (c + 1) * size, :], preferred_element_type=jnp.float32)
        block = block.astype(jnp.bfloat16)
        for p in range(parts):
            rows_in[p, c * each : (c + 1) * each, :] = block[p * each : (p + 1) * each]
    tile = 256
    for c in range(0, inner, tile):
        gate = jnp.zeros((slots, tile), jnp.float32)
        up = jnp.zeros((slots, tile), jnp.float32)
        for p in range(parts):
            deep_part = slice(p * piece, (p + 1) * piece)
            gate = gate + jnp.dot(rows_in[p], first[0, deep_part, c : c + tile], preferred_element_type=jnp.float32)
            up = up + jnp.dot(
                rows_in[p], first[0, deep_part, inner + c : inner + c + tile], preferred_element_type=jnp.float32
            )
        hidden[:, c : c + tile] = (gate / (1.0 + jnp.exp(-gate)) * up).astype(jnp.bfloat16)
    for p in range(parts):
        rows_out[p] = jnp.dot(
            hidden[...], second[0, :, p * piece : (p + 1) * piece], preferred_element_type=jnp.float32
        ).astype(jnp.bfloat16)
    back = regroup(True)
    for c in range(out_ref.shape[0] // size):
        block = jnp.concatenate([rows_out[p, c * each : (c + 1) * each, :] for p in range(parts)], axis=0)
        block = jnp.dot(back, block, preferred_element_type=jnp.float32)
        out_ref[c * size : (c + 1) * size, :] = block.astype(jnp.bfloat16)


def body(states, routes, gate_scores, w_in, w_out):
    rows, width = states.shape
    experts = lax.axis_size(axes)
    piece = width // parts
    columns = experts * lines
    slots = experts * most
    _, deep, both = w_in.shape
    inner = w_out.shape[1]
    work = 2 * slots * width * inner * 3
    weights = 2 * width * inner * 3
    vmem = pl.BlockSpec(memory_space=pltpu.VMEM)
    message = jax.ShapeDtypeStruct((columns, piece), jnp.bfloat16)

    outgoing = pl.pallas_call(
        dispatch_kernel,
        out_shape=message,
        in_specs=[vmem] * 2,
        out_specs=vmem,
        compiler_params=pltpu.CompilerParams(vmem_limit_bytes=8 << 20),
        cost_estimate=pl.CostEstimate(flops=16 * work, bytes_accessed=8 * weights, transcendentals=0),
        name="dispatch",
    )(routes.T, states)
    received = lax.all_to_all(outgoing, axes, split_axis=0, concat_axis=0, tiled=True)
    result = pl.pallas_call(
        ffn_kernel,
        out_shape=message,
        in_specs=[vmem] * 3,
        out_specs=vmem,
        scratch_shapes=[
            pltpu.VMEM((parts, slots, piece), jnp.bfloat16),
            pltpu.VMEM((slots, inner), jnp.bfloat16),
            pltpu.VMEM((parts, slots, piece), jnp.bfloat16),
        ],
        compiler_params=pltpu.CompilerParams(vmem_limit_bytes=16 << 20),
        cost_estimate=pl.CostEstimate(
            flops=work, bytes_accessed=weights, transcendentals=slots * inner
        ),
        name="expert_ffn",
    )(received, w_in, w_out)
    returned = lax.all_to_all(result, axes, split_axis=0, concat_axis=0, tiled=True)
    return pl.pallas_call(
        combine_kernel,
        out_shape=jax.ShapeDtypeStruct((rows, width), jnp.bfloat16),
        in_specs=[vmem] * 4,
        out_specs=vmem,
        compiler_params=pltpu.CompilerParams(vmem_limit_bytes=24 << 20),
        name="combine",
    )(routes.T, gate_scores.T, states, returned)


def solution(mesh):
    return jax.shard_map(
        body,
        mesh=mesh,
        in_specs=(
            P(axes, None),
            P(axes, None),
            P(axes, None),
            P(axes, None, None),
            P(axes, None, None),
        ),
        out_specs=P(axes, None),
        check_vma=False,
    )
```

```python
import functools

import jax
import jax.numpy as jnp
from jax import lax
from jax.experimental import pallas as pl
from jax.experimental.pallas import tpu as pltpu
from jax.sharding import PartitionSpec as P

route_scale = 2.5
axes = ("grp", "dev")
most = 2
parts = 4
lines = most * parts
group = 16


def slot_of(routes, columns):
    rows, top = routes.shape
    column = lax.broadcasted_iota(jnp.int32, (rows, columns), 1)
    expert = column // lines
    named = jnp.zeros((rows, columns), jnp.float32)
    for k in range(top):
        named = named + (routes[:, k : k + 1] == expert).astype(jnp.float32)
    earlier = (
        lax.broadcasted_iota(jnp.int32, (rows, rows), 0)
        > lax.broadcasted_iota(jnp.int32, (rows, rows), 1)
    ).astype(jnp.float32)
    position = jnp.dot(earlier, named, preferred_element_type=jnp.float32)
    slot = (column % most).astype(jnp.float32)
    return expert, (named > 0.5) & (jnp.abs(position - slot) < 0.5), column // most % parts


def pick_kernel(routes_ref, pick_ref):
    _, filled, part = slot_of(routes_ref[...].T, pick_ref.shape[1])
    pick_ref[...] = jnp.concatenate(
        [(filled & (part == p)).astype(jnp.float32) for p in range(parts)], axis=0
    ).astype(jnp.bfloat16)


def dispatch_kernel(pick_ref, states_ref, out_ref):
    columns, piece = out_ref.shape
    source = jnp.concatenate(
        [states_ref[:, p * piece : (p + 1) * piece] for p in range(parts)], axis=0
    )
    step = 128
    for c in range(0, columns, step):
        block = lax.dot_general(
            pick_ref[:, c : c + step],
            source,
            (((0,), (0,)), ((), ())),
            preferred_element_type=jnp.float32,
        )
        out_ref[c : c + step, :] = block.astype(jnp.bfloat16)


def combine_kernel(routes_ref, scores_ref, states_ref, got_ref, out_ref):
    rows, width = states_ref.shape
    columns, piece = got_ref.shape
    routes = routes_ref[...].T
    scores = scores_ref[...].T
    weights = scores / jnp.sum(scores, axis=1, keepdims=True) * route_scale
    expert, filled, part = slot_of(routes, columns)
    weight = jnp.zeros((rows, columns), jnp.float32)
    for k in range(routes.shape[1]):
        weight = weight + jnp.where(routes[:, k : k + 1] == expert, weights[:, k : k + 1], 0.0)
    weight = jnp.where(filled, weight, 0.0)
    high = weight.astype(jnp.bfloat16).astype(jnp.float32)
    low = weight - high
    mix = jnp.concatenate(
        [jnp.where(part == p, w, 0.0) for w in (high, low) for p in range(parts)], axis=0
    ).astype(jnp.bfloat16)
    total = jnp.dot(mix, got_ref[...], preferred_element_type=jnp.float32)
    for p in range(parts):
        both = total[p * rows : (p + 1) * rows] + total[(parts + p) * rows : (parts + p + 1) * rows]
        own = states_ref[:, p * piece : (p + 1) * piece].astype(jnp.float32)
        out_ref[:, p * piece : (p + 1) * piece] = (own + both).astype(jnp.bfloat16)


def regroup(inverse):
    size = group * lines
    there = lax.broadcasted_iota(jnp.int32, (size, size), 1 if inverse else 0)
    here = lax.broadcasted_iota(jnp.int32, (size, size), 0 if inverse else 1)
    part = there // (group * most)
    message = there % (group * most) // most
    match = here == message * lines + part * most + there % most
    return match.astype(jnp.float32).astype(jnp.bfloat16)


def ffn_kernel(in_ref, first, second, out_ref, rows_in, hidden, rows_out):
    inner, width = second.shape[1:]
    piece = in_ref.shape[1]
    size = group * lines
    each = group * most
    order = regroup(False)
    for c in range(in_ref.shape[0] // size):
        block = jnp.dot(order, in_ref[c * size : (c + 1) * size, :], preferred_element_type=jnp.float32)
        block = block.astype(jnp.bfloat16)
        for p in range(parts):
            rows_in[c * each : (c + 1) * each, p * piece : (p + 1) * piece] = block[p * each : (p + 1) * each]
    tile = 256
    for c in range(0, inner, tile):
        gate = jnp.dot(rows_in[...], first[0, :, c : c + tile], preferred_element_type=jnp.float32)
        up = jnp.dot(
            rows_in[...], first[0, :, inner + c : inner + c + tile], preferred_element_type=jnp.float32
        )
        hidden[:, c : c + tile] = (gate / (1.0 + jnp.exp(-gate)) * up).astype(jnp.bfloat16)
    tile = 512
    for c in range(0, width, tile):
        rows_out[:, c : c + tile] = jnp.dot(
            hidden[...], second[0, :, c : c + tile], preferred_element_type=jnp.float32
        ).astype(jnp.bfloat16)
    back = regroup(True)
    for c in range(out_ref.shape[0] // size):
        block = jnp.concatenate(
            [rows_out[c * each : (c + 1) * each, p * piece : (p + 1) * piece] for p in range(parts)], axis=0
        )
        block = jnp.dot(back, block, preferred_element_type=jnp.float32)
        out_ref[c * size : (c + 1) * size, :] = block.astype(jnp.bfloat16)


def body(states, routes, gate_scores, w_in, w_out):
    rows, width = states.shape
    experts = lax.axis_size(axes)
    piece = width // parts
    columns = experts * lines
    slots = experts * most
    _, deep, both = w_in.shape
    inner = w_out.shape[1]
    work = 2 * slots * width * inner * 3
    weights = 2 * width * inner * 3
    vmem = pl.BlockSpec(memory_space=pltpu.VMEM)
    message = jax.ShapeDtypeStruct((columns, piece), jnp.bfloat16)

    pick = pl.pallas_call(
        pick_kernel,
        out_shape=jax.ShapeDtypeStruct((parts * rows, columns), jnp.bfloat16),
        in_specs=[vmem],
        out_specs=vmem,
        compiler_params=pltpu.CompilerParams(vmem_limit_bytes=8 << 20),
        cost_estimate=pl.CostEstimate(flops=16 * work, bytes_accessed=8 * weights, transcendentals=0),
        name="pick",
    )(routes.T)
    outgoing = pl.pallas_call(
        dispatch_kernel,
        out_shape=message,
        in_specs=[vmem] * 2,
        out_specs=vmem,
        compiler_params=pltpu.CompilerParams(vmem_limit_bytes=8 << 20),
        name="dispatch",
    )(pick, states)
    received = lax.all_to_all(outgoing, axes, split_axis=0, concat_axis=0, tiled=True)
    result = pl.pallas_call(
        ffn_kernel,
        out_shape=message,
        in_specs=[vmem] * 3,
        out_specs=vmem,
        scratch_shapes=[
            pltpu.VMEM((slots, width), jnp.bfloat16),
            pltpu.VMEM((slots, inner), jnp.bfloat16),
            pltpu.VMEM((slots, width), jnp.bfloat16),
        ],
        compiler_params=pltpu.CompilerParams(vmem_limit_bytes=16 << 20),
        cost_estimate=pl.CostEstimate(
            flops=work, bytes_accessed=weights, transcendentals=slots * inner
        ),
        name="expert_ffn",
    )(received, w_in, w_out)
    returned = lax.all_to_all(result, axes, split_axis=0, concat_axis=0, tiled=True)
    return pl.pallas_call(
        combine_kernel,
        out_shape=jax.ShapeDtypeStruct((rows, width), jnp.bfloat16),
        in_specs=[vmem] * 4,
        out_specs=vmem,
        compiler_params=pltpu.CompilerParams(vmem_limit_bytes=24 << 20),
        name="combine",
    )(routes.T, gate_scores.T, states, returned)


def solution(mesh):
    return jax.shard_map(
        body,
        mesh=mesh,
        in_specs=(
            P(axes, None),
            P(axes, None),
            P(axes, None),
            P(axes, None, None),
            P(axes, None, None),
        ),
        out_specs=P(axes, None),
        check_vma=False,
    )
```

```python
import jax
import jax.numpy as jnp
from jax import lax
from jax.experimental import pallas as pl
from jax.experimental.pallas import tpu as pltpu
from jax.sharding import PartitionSpec as P

route_scale = 2.5
axes = ("grp", "dev")
most = 2
parts = 4
lines = most * parts
group = 16


def column_kernel(expert_ref):
    expert_ref[...] = lax.broadcasted_iota(jnp.int32, expert_ref.shape, 1) // lines


def slot_of(routes, expert):
    rows, top = routes.shape
    column = lax.broadcasted_iota(jnp.int32, expert.shape, 1)
    named = jnp.zeros(expert.shape, jnp.float32)
    for k in range(top):
        named = named + (routes[:, k : k + 1] == expert).astype(jnp.float32)
    earlier = (
        lax.broadcasted_iota(jnp.int32, (rows, rows), 0)
        > lax.broadcasted_iota(jnp.int32, (rows, rows), 1)
    ).astype(jnp.float32)
    position = jnp.dot(earlier, named, preferred_element_type=jnp.float32)
    slot = (column % most).astype(jnp.float32)
    return (named > 0.5) & (jnp.abs(position - slot) < 0.5), column // most % parts


def pick_kernel(routes_ref, expert_ref, pick_ref):
    filled, part = slot_of(routes_ref[...].T, expert_ref[...])
    pick_ref[...] = jnp.concatenate(
        [(filled & (part == p)).astype(jnp.float32) for p in range(parts)], axis=0
    ).astype(jnp.bfloat16)


def dispatch_kernel(pick_ref, states_ref, out_ref):
    columns, piece = out_ref.shape
    source = jnp.concatenate(
        [states_ref[:, p * piece : (p + 1) * piece] for p in range(parts)], axis=0
    )
    step = 128
    for c in range(0, columns, step):
        block = lax.dot_general(
            pick_ref[:, c : c + step],
            source,
            (((0,), (0,)), ((), ())),
            preferred_element_type=jnp.float32,
        )
        out_ref[c : c + step, :] = block.astype(jnp.bfloat16)


def mix_of(routes, scores, pick, expert):
    weights = scores / jnp.sum(scores, axis=1, keepdims=True) * route_scale
    weight = jnp.zeros(expert.shape, jnp.float32)
    for k in range(routes.shape[1]):
        weight = jnp.where(routes[:, k : k + 1] == expert, weights[:, k : k + 1], weight)
    high = weight.astype(jnp.bfloat16)
    low = (weight - high.astype(jnp.float32)).astype(jnp.bfloat16)
    return jnp.concatenate([pick * jnp.concatenate([w] * parts, axis=0) for w in (high, low)], axis=0)


def combine_kernel(routes_ref, scores_ref, pick_ref, expert_ref, states_ref, got_ref, out_ref):
    rows, width = states_ref.shape
    columns, piece = got_ref.shape
    mix = mix_of(routes_ref[...].T, scores_ref[...].T, pick_ref[...], expert_ref[...])
    total = jnp.dot(mix, got_ref[...], preferred_element_type=jnp.float32)
    for p in range(parts):
        both = total[p * rows : (p + 1) * rows] + total[(parts + p) * rows : (parts + p + 1) * rows]
        own = states_ref[:, p * piece : (p + 1) * piece].astype(jnp.float32)
        out_ref[:, p * piece : (p + 1) * piece] = (own + both).astype(jnp.bfloat16)


def regroup(inverse):
    size = group * lines
    there = lax.broadcasted_iota(jnp.int32, (size, size), 1 if inverse else 0)
    here = lax.broadcasted_iota(jnp.int32, (size, size), 0 if inverse else 1)
    part = there // (group * most)
    message = there % (group * most) // most
    match = here == message * lines + part * most + there % most
    return match.astype(jnp.float32).astype(jnp.bfloat16)


def ffn_kernel(in_ref, first, second, out_ref, rows_in, hidden, rows_out):
    inner, width = second.shape[1:]
    piece = in_ref.shape[1]
    size = group * lines
    each = group * most
    order = regroup(False)
    for c in range(in_ref.shape[0] // size):
        block = jnp.dot(order, in_ref[c * size : (c + 1) * size, :], preferred_element_type=jnp.float32)
        block = block.astype(jnp.bfloat16)
        for p in range(parts):
            rows_in[c * each : (c + 1) * each, p * piece : (p + 1) * piece] = block[p * each : (p + 1) * each]
    tile = 256
    for c in range(0, inner, tile):
        gate = jnp.dot(rows_in[...], first[0, :, c : c + tile], preferred_element_type=jnp.float32)
        up = jnp.dot(
            rows_in[...], first[0, :, inner + c : inner + c + tile], preferred_element_type=jnp.float32
        )
        hidden[:, c : c + tile] = (gate / (1.0 + jnp.exp(-gate)) * up).astype(jnp.bfloat16)
    tile = 512
    for c in range(0, width, tile):
        rows_out[:, c : c + tile] = jnp.dot(
            hidden[...], second[0, :, c : c + tile], preferred_element_type=jnp.float32
        ).astype(jnp.bfloat16)
    back = regroup(True)
    for c in range(out_ref.shape[0] // size):
        block = jnp.concatenate(
            [rows_out[c * each : (c + 1) * each, p * piece : (p + 1) * piece] for p in range(parts)], axis=0
        )
        block = jnp.dot(back, block, preferred_element_type=jnp.float32)
        out_ref[c * size : (c + 1) * size, :] = block.astype(jnp.bfloat16)


def body(states, routes, gate_scores, w_in, w_out):
    rows, width = states.shape
    experts = lax.axis_size(axes)
    piece = width // parts
    columns = experts * lines
    slots = experts * most
    inner = w_out.shape[1]
    work = 2 * slots * width * inner * 3
    weights = 2 * width * inner * 3
    vmem = pl.BlockSpec(memory_space=pltpu.VMEM)
    message = jax.ShapeDtypeStruct((columns, piece), jnp.bfloat16)
    small = pltpu.CompilerParams(vmem_limit_bytes=8 << 20)

    expert = pl.pallas_call(
        column_kernel,
        out_shape=jax.ShapeDtypeStruct((rows, columns), jnp.int32),
        out_specs=vmem,
        compiler_params=small,
        cost_estimate=pl.CostEstimate(flops=16 * work, bytes_accessed=8 * weights, transcendentals=0),
        name="columns",
    )()
    pick = pl.pallas_call(
        pick_kernel,
        out_shape=jax.ShapeDtypeStruct((parts * rows, columns), jnp.bfloat16),
        in_specs=[vmem] * 2,
        out_specs=vmem,
        compiler_params=small,
        name="pick",
    )(routes.T, expert)
    outgoing = pl.pallas_call(
        dispatch_kernel,
        out_shape=message,
        in_specs=[vmem] * 2,
        out_specs=vmem,
        compiler_params=small,
        name="dispatch",
    )(pick, states)
    received = lax.all_to_all(outgoing, axes, split_axis=0, concat_axis=0, tiled=True)
    result = pl.pallas_call(
        ffn_kernel,
        out_shape=message,
        in_specs=[vmem] * 3,
        out_specs=vmem,
        scratch_shapes=[
            pltpu.VMEM((slots, width), jnp.bfloat16),
            pltpu.VMEM((slots, inner), jnp.bfloat16),
            pltpu.VMEM((slots, width), jnp.bfloat16),
        ],
        compiler_params=pltpu.CompilerParams(vmem_limit_bytes=16 << 20),
        cost_estimate=pl.CostEstimate(
            flops=work, bytes_accessed=weights, transcendentals=slots * inner
        ),
        name="expert_ffn",
    )(received, w_in, w_out)
    returned = lax.all_to_all(result, axes, split_axis=0, concat_axis=0, tiled=True)
    return pl.pallas_call(
        combine_kernel,
        out_shape=jax.ShapeDtypeStruct((rows, width), jnp.bfloat16),
        in_specs=[vmem] * 6,
        out_specs=vmem,
        compiler_params=small,
        name="combine",
    )(routes.T, gate_scores.T, pick, expert, states, returned)


def solution(mesh):
    return jax.shard_map(
        body,
        mesh=mesh,
        in_specs=(
            P(axes, None),
            P(axes, None),
            P(axes, None),
            P(axes, None, None),
            P(axes, None, None),
        ),
        out_specs=P(axes, None),
        check_vma=False,
    )
```

```python
import jax
import jax.numpy as jnp
from jax import lax
from jax.experimental import pallas as pl
from jax.experimental.pallas import tpu as pltpu
from jax.sharding import PartitionSpec as P

route_scale = 2.5
axes = ("grp", "dev")
most = 2


def column_kernel(expert_ref):
    expert_ref[...] = lax.broadcasted_iota(jnp.int32, expert_ref.shape, 1) // most


def pick_kernel(routes_ref, expert_ref, pick_ref):
    routes = routes_ref[...].T
    expert = expert_ref[...]
    rows, top = routes.shape
    named = jnp.zeros(expert.shape, jnp.float32)
    for k in range(top):
        named = named + (routes[:, k : k + 1] == expert).astype(jnp.float32)
    earlier = (
        lax.broadcasted_iota(jnp.int32, (rows, rows), 0)
        > lax.broadcasted_iota(jnp.int32, (rows, rows), 1)
    ).astype(jnp.float32)
    position = jnp.dot(earlier, named, preferred_element_type=jnp.float32)
    slot = (lax.broadcasted_iota(jnp.int32, expert.shape, 1) % most).astype(jnp.float32)
    filled = (named > 0.5) & (jnp.abs(position - slot) < 0.5)
    pick_ref[...] = filled.astype(jnp.float32).astype(jnp.bfloat16)


def dispatch_kernel(pick_ref, states_ref, out_ref):
    experts, _, width = out_ref.shape
    tile = 512
    for c in range(0, width, tile):
        block = lax.dot_general(
            pick_ref[...],
            states_ref[:, c : c + tile],
            (((0,), (0,)), ((), ())),
            preferred_element_type=jnp.float32,
        )
        out_ref[:, :, c : c + tile] = block.astype(jnp.bfloat16).reshape(experts, most, tile)


def ffn_kernel(in_ref, first, second, out_ref, rows_in, hidden):
    inner, width = second.shape[1:]
    rows_in[...] = in_ref[...].reshape(rows_in.shape)
    tile = 256
    for c in range(0, inner, tile):
        gate = jnp.dot(rows_in[...], first[0, :, c : c + tile], preferred_element_type=jnp.float32)
        up = jnp.dot(
            rows_in[...], first[0, :, inner + c : inner + c + tile], preferred_element_type=jnp.float32
        )
        hidden[:, c : c + tile] = (gate / (1.0 + jnp.exp(-gate)) * up).astype(jnp.bfloat16)
    tile = 512
    for c in range(0, width, tile):
        block = jnp.dot(hidden[...], second[0, :, c : c + tile], preferred_element_type=jnp.float32)
        out_ref[:, :, c : c + tile] = block.astype(jnp.bfloat16).reshape(-1, most, tile)


def combine_kernel(routes_ref, scores_ref, pick_ref, expert_ref, states_ref, got_ref, out_ref):
    rows, width = states_ref.shape
    routes = routes_ref[...].T
    scores = scores_ref[...].T
    expert = expert_ref[...]
    pick = pick_ref[...]
    weights = scores / jnp.sum(scores, axis=1, keepdims=True) * route_scale
    weight = jnp.zeros(expert.shape, jnp.float32)
    for k in range(routes.shape[1]):
        weight = jnp.where(routes[:, k : k + 1] == expert, weights[:, k : k + 1], weight)
    high = weight.astype(jnp.bfloat16)
    low = (weight - high.astype(jnp.float32)).astype(jnp.bfloat16)
    mix = jnp.concatenate([pick * high, pick * low], axis=0)
    total = jnp.dot(mix, got_ref[...].reshape(-1, width), preferred_element_type=jnp.float32)
    out_ref[...] = (states_ref[...].astype(jnp.float32) + (total[:rows] + total[rows:])).astype(jnp.bfloat16)


def body(states, routes, gate_scores, w_in, w_out):
    rows, width = states.shape
    experts = lax.axis_size(axes)
    slots = experts * most
    inner = w_out.shape[1]
    work = 2 * slots * width * inner * 3
    weights = 2 * width * inner * 3
    vmem = pl.BlockSpec(memory_space=pltpu.VMEM)
    message = jax.ShapeDtypeStruct((experts, most, width), jnp.bfloat16)
    small = pltpu.CompilerParams(vmem_limit_bytes=8 << 20)

    expert = pl.pallas_call(
        column_kernel,
        out_shape=jax.ShapeDtypeStruct((rows, slots), jnp.int32),
        out_specs=vmem,
        compiler_params=small,
        cost_estimate=pl.CostEstimate(flops=16 * work, bytes_accessed=8 * weights, transcendentals=0),
        name="columns",
    )()
    pick = pl.pallas_call(
        pick_kernel,
        out_shape=jax.ShapeDtypeStruct((rows, slots), jnp.bfloat16),
        in_specs=[vmem] * 2,
        out_specs=vmem,
        compiler_params=small,
        name="pick",
    )(routes.T, expert)
    outgoing = pl.pallas_call(
        dispatch_kernel,
        out_shape=message,
        in_specs=[vmem] * 2,
        out_specs=vmem,
        compiler_params=small,
        name="dispatch",
    )(pick, states)
    received = lax.all_to_all(outgoing, axes, split_axis=0, concat_axis=0, tiled=True)
    result = pl.pallas_call(
        ffn_kernel,
        out_shape=message,
        in_specs=[vmem] * 3,
        out_specs=vmem,
        scratch_shapes=[
            pltpu.VMEM((slots, width), jnp.bfloat16),
            pltpu.VMEM((slots, inner), jnp.bfloat16),
        ],
        compiler_params=pltpu.CompilerParams(vmem_limit_bytes=16 << 20),
        cost_estimate=pl.CostEstimate(
            flops=work, bytes_accessed=weights, transcendentals=slots * inner
        ),
        name="expert_ffn",
    )(received, w_in, w_out)
    returned = lax.all_to_all(result, axes, split_axis=0, concat_axis=0, tiled=True)
    return pl.pallas_call(
        combine_kernel,
        out_shape=jax.ShapeDtypeStruct((rows, width), jnp.bfloat16),
        in_specs=[vmem] * 6,
        out_specs=vmem,
        compiler_params=small,
        name="combine",
    )(routes.T, gate_scores.T, pick, expert, states, returned)


def solution(mesh):
    return jax.shard_map(
        body,
        mesh=mesh,
        in_specs=(
            P(axes, None),
            P(axes, None),
            P(axes, None),
            P(axes, None, None),
            P(axes, None, None),
        ),
        out_specs=P(axes, None),
        check_vma=False,
    )
```

```python
import functools

import jax
import jax.numpy as jnp
from jax import lax
from jax.experimental import pallas as pl
from jax.experimental.pallas import tpu as pltpu
from jax.sharding import Mesh
from jax.sharding import PartitionSpec as P

route_scale = 2.5
axes = ("grp", "x", "y", "z")
turn = ("grp", "z", "y", "x")
most = 2


def column_kernel(sizes, expert_ref):
    left = lax.broadcasted_iota(jnp.int32, expert_ref.shape, 1) // most
    place = {}
    for axis in reversed(turn):
        place[axis] = left % sizes[axis]
        left = left // sizes[axis]
    expert = jnp.zeros_like(left)
    for axis in axes:
        expert = expert * sizes[axis] + place[axis]
    expert_ref[...] = expert


def pick_kernel(routes_ref, expert_ref, pick_ref):
    routes = routes_ref[...].T
    expert = expert_ref[...]
    rows, top = routes.shape
    named = jnp.zeros(expert.shape, jnp.float32)
    for k in range(top):
        named = named + (routes[:, k : k + 1] == expert).astype(jnp.float32)
    earlier = (
        lax.broadcasted_iota(jnp.int32, (rows, rows), 0)
        > lax.broadcasted_iota(jnp.int32, (rows, rows), 1)
    ).astype(jnp.float32)
    position = jnp.dot(earlier, named, preferred_element_type=jnp.float32)
    slot = (lax.broadcasted_iota(jnp.int32, expert.shape, 1) % most).astype(jnp.float32)
    filled = (named > 0.5) & (jnp.abs(position - slot) < 0.5)
    pick_ref[...] = filled.astype(jnp.float32).astype(jnp.bfloat16)


def dispatch_kernel(pick_ref, states_ref, out_ref):
    experts, _, width = out_ref.shape
    tile = 512
    for c in range(0, width, tile):
        block = lax.dot_general(
            pick_ref[...],
            states_ref[:, c : c + tile],
            (((0,), (0,)), ((), ())),
            preferred_element_type=jnp.float32,
        )
        out_ref[:, :, c : c + tile] = block.astype(jnp.bfloat16).reshape(experts, most, tile)


def ffn_kernel(in_ref, first, second, out_ref, rows_in, hidden):
    inner, width = second.shape[1:]
    rows_in[...] = in_ref[...].reshape(rows_in.shape)
    tile = 256
    for c in range(0, inner, tile):
        gate = jnp.dot(rows_in[...], first[0, :, c : c + tile], preferred_element_type=jnp.float32)
        up = jnp.dot(
            rows_in[...], first[0, :, inner + c : inner + c + tile], preferred_element_type=jnp.float32
        )
        hidden[:, c : c + tile] = (gate / (1.0 + jnp.exp(-gate)) * up).astype(jnp.bfloat16)
    tile = 512
    for c in range(0, width, tile):
        block = jnp.dot(hidden[...], second[0, :, c : c + tile], preferred_element_type=jnp.float32)
        out_ref[:, :, c : c + tile] = block.astype(jnp.bfloat16).reshape(-1, most, tile)


def combine_kernel(routes_ref, scores_ref, pick_ref, expert_ref, states_ref, got_ref, out_ref):
    rows, width = states_ref.shape
    routes = routes_ref[...].T
    scores = scores_ref[...].T
    expert = expert_ref[...]
    pick = pick_ref[...]
    weights = scores / jnp.sum(scores, axis=1, keepdims=True) * route_scale
    weight = jnp.zeros(expert.shape, jnp.float32)
    for k in range(routes.shape[1]):
        weight = jnp.where(routes[:, k : k + 1] == expert, weights[:, k : k + 1], weight)
    high = weight.astype(jnp.bfloat16)
    low = (weight - high.astype(jnp.float32)).astype(jnp.bfloat16)
    mix = jnp.concatenate([pick * high, pick * low], axis=0)
    total = jnp.dot(mix, got_ref[...].reshape(-1, width), preferred_element_type=jnp.float32)
    out_ref[...] = (states_ref[...].astype(jnp.float32) + (total[:rows] + total[rows:])).astype(jnp.bfloat16)


def body(states, routes, gate_scores, w_in, w_out):
    rows, width = states.shape
    experts = lax.axis_size(axes)
    slots = experts * most
    inner = w_out.shape[1]
    work = 2 * slots * width * inner * 3
    weights = 2 * width * inner * 3
    vmem = pl.BlockSpec(memory_space=pltpu.VMEM)
    message = jax.ShapeDtypeStruct((experts, most, width), jnp.bfloat16)
    small = pltpu.CompilerParams(vmem_limit_bytes=8 << 20)

    expert = pl.pallas_call(
        functools.partial(column_kernel, {axis: lax.axis_size(axis) for axis in axes}),
        out_shape=jax.ShapeDtypeStruct((rows, slots), jnp.int32),
        out_specs=vmem,
        compiler_params=small,
        cost_estimate=pl.CostEstimate(flops=16 * work, bytes_accessed=8 * weights, transcendentals=0),
        name="columns",
    )()
    pick = pl.pallas_call(
        pick_kernel,
        out_shape=jax.ShapeDtypeStruct((rows, slots), jnp.bfloat16),
        in_specs=[vmem] * 2,
        out_specs=vmem,
        compiler_params=small,
        name="pick",
    )(routes.T, expert)
    outgoing = pl.pallas_call(
        dispatch_kernel,
        out_shape=message,
        in_specs=[vmem] * 2,
        out_specs=vmem,
        compiler_params=small,
        name="dispatch",
    )(pick, states)
    received = lax.all_to_all(outgoing, turn, split_axis=0, concat_axis=0, tiled=True)
    result = pl.pallas_call(
        ffn_kernel,
        out_shape=message,
        in_specs=[vmem] * 3,
        out_specs=vmem,
        scratch_shapes=[
            pltpu.VMEM((slots, width), jnp.bfloat16),
            pltpu.VMEM((slots, inner), jnp.bfloat16),
        ],
        compiler_params=pltpu.CompilerParams(vmem_limit_bytes=16 << 20),
        cost_estimate=pl.CostEstimate(
            flops=work, bytes_accessed=weights, transcendentals=slots * inner
        ),
        name="expert_ffn",
    )(received, w_in, w_out)
    returned = lax.all_to_all(result, turn, split_axis=0, concat_axis=0, tiled=True)
    return pl.pallas_call(
        combine_kernel,
        out_shape=jax.ShapeDtypeStruct((rows, width), jnp.bfloat16),
        in_specs=[vmem] * 6,
        out_specs=vmem,
        compiler_params=small,
        name="combine",
    )(routes.T, gate_scores.T, pick, expert, states, returned)


def solution(mesh):
    cores, chips = mesh.devices.shape
    side = round(chips ** (1 / 3))
    return jax.shard_map(
        body,
        mesh=Mesh(mesh.devices.reshape(cores, side, side, side), axes),
        in_specs=(
            P(axes, None),
            P(axes, None),
            P(axes, None),
            P(axes, None, None),
            P(axes, None, None),
        ),
        out_specs=P(axes, None),
        check_vma=False,
    )
```

```python
import functools

import jax
import jax.numpy as jnp
from jax import lax
from jax.experimental import pallas as pl
from jax.experimental.pallas import tpu as pltpu
from jax.sharding import Mesh
from jax.sharding import PartitionSpec as P

route_scale = 2.5
axes = ("grp", "x", "y", "z")
turn = ("grp", "z", "y", "x")
most = 2


def column_kernel(sizes, expert_ref):
    left = lax.broadcasted_iota(jnp.int32, expert_ref.shape, 0) // most
    place = {}
    for axis in reversed(turn):
        place[axis] = left % sizes[axis]
        left = left // sizes[axis]
    expert = jnp.zeros_like(left)
    for axis in axes:
        expert = expert * sizes[axis] + place[axis]
    expert_ref[...] = expert


def pick_kernel(routes_ref, expert_ref, pick_ref):
    expert = expert_ref[...]
    top, rows = routes_ref.shape
    named = jnp.zeros(expert.shape, jnp.float32)
    for k in range(top):
        named = jnp.where(routes_ref[k : k + 1, :] == expert, 1.0, named)
    earlier = (
        lax.broadcasted_iota(jnp.int32, (rows, rows), 0)
        < lax.broadcasted_iota(jnp.int32, (rows, rows), 1)
    ).astype(jnp.float32)
    position = jnp.dot(
        named.astype(jnp.bfloat16), earlier.astype(jnp.bfloat16), preferred_element_type=jnp.float32
    )
    slot = (lax.broadcasted_iota(jnp.int32, expert.shape, 0) % most).astype(jnp.float32)
    pick_ref[...] = jnp.where(jnp.abs(position - slot) < 0.5, named, 0.0).astype(jnp.bfloat16)


def dispatch_kernel(pick_ref, states_ref, out_ref):
    experts, _, width = out_ref.shape
    tile = 512
    for c in range(0, width, tile):
        block = jnp.dot(pick_ref[...], states_ref[:, c : c + tile], preferred_element_type=jnp.float32)
        out_ref[:, :, c : c + tile] = block.astype(jnp.bfloat16).reshape(experts, most, tile)


def ffn_kernel(in_ref, first, second, out_ref, rows_in, hidden):
    inner, width = second.shape[1:]
    rows_in[...] = in_ref[...].reshape(rows_in.shape)
    tile = 256
    for c in range(0, inner, tile):
        gate = jnp.dot(rows_in[...], first[0, :, c : c + tile], preferred_element_type=jnp.float32)
        up = jnp.dot(
            rows_in[...], first[0, :, inner + c : inner + c + tile], preferred_element_type=jnp.float32
        )
        hidden[:, c : c + tile] = (gate / (1.0 + jnp.exp(-gate)) * up).astype(jnp.bfloat16)
    tile = 512
    for c in range(0, width, tile):
        block = jnp.dot(hidden[...], second[0, :, c : c + tile], preferred_element_type=jnp.float32)
        out_ref[:, :, c : c + tile] = block.astype(jnp.bfloat16).reshape(-1, most, tile)


def combine_kernel(routes_ref, scores_ref, pick_ref, expert_ref, states_ref, got_ref, out_ref):
    rows, width = states_ref.shape
    scores = scores_ref[...]
    expert = expert_ref[...]
    pick = pick_ref[...]
    weights = scores / jnp.sum(scores, axis=0, keepdims=True) * route_scale
    weight = jnp.zeros(expert.shape, jnp.float32)
    for k in range(routes_ref.shape[0]):
        weight = jnp.where(routes_ref[k : k + 1, :] == expert, weights[k : k + 1, :], weight)
    high = weight.astype(jnp.bfloat16)
    low = (weight - high.astype(jnp.float32)).astype(jnp.bfloat16)
    got = got_ref[...].reshape(-1, width)
    mix = jnp.concatenate([pick * high, pick * low], axis=1)
    total = lax.dot_general(mix, got, (((0,), (0,)), ((), ())), preferred_element_type=jnp.float32)
    total = total[:rows] + total[rows:]
    out_ref[...] = (states_ref[...].astype(jnp.float32) + total).astype(jnp.bfloat16)


def body(states, routes, gate_scores, w_in, w_out):
    rows, width = states.shape
    experts = lax.axis_size(axes)
    slots = experts * most
    inner = w_out.shape[1]
    work = 2 * slots * width * inner * 3
    weights = 2 * width * inner * 3
    vmem = pl.BlockSpec(memory_space=pltpu.VMEM)
    message = jax.ShapeDtypeStruct((experts, most, width), jnp.bfloat16)
    small = pltpu.CompilerParams(vmem_limit_bytes=8 << 20)

    expert = pl.pallas_call(
        functools.partial(column_kernel, {axis: lax.axis_size(axis) for axis in axes}),
        out_shape=jax.ShapeDtypeStruct((slots, rows), jnp.int32),
        out_specs=vmem,
        compiler_params=small,
        cost_estimate=pl.CostEstimate(flops=16 * work, bytes_accessed=8 * weights, transcendentals=0),
        name="columns",
    )()
    pick = pl.pallas_call(
        pick_kernel,
        out_shape=jax.ShapeDtypeStruct((slots, rows), jnp.bfloat16),
        in_specs=[vmem] * 2,
        out_specs=vmem,
        compiler_params=small,
        name="pick",
    )(routes.T, expert)
    outgoing = pl.pallas_call(
        dispatch_kernel,
        out_shape=message,
        in_specs=[vmem] * 2,
        out_specs=vmem,
        compiler_params=small,
        name="dispatch",
    )(pick, states)
    received = lax.all_to_all(outgoing, turn, split_axis=0, concat_axis=0, tiled=True)
    result = pl.pallas_call(
        ffn_kernel,
        out_shape=message,
        in_specs=[vmem] * 3,
        out_specs=vmem,
        scratch_shapes=[
            pltpu.VMEM((slots, width), jnp.bfloat16),
            pltpu.VMEM((slots, inner), jnp.bfloat16),
        ],
        compiler_params=pltpu.CompilerParams(vmem_limit_bytes=16 << 20),
        cost_estimate=pl.CostEstimate(
            flops=work, bytes_accessed=weights, transcendentals=slots * inner
        ),
        name="expert_ffn",
    )(received, w_in, w_out)
    returned = lax.all_to_all(result, turn, split_axis=0, concat_axis=0, tiled=True)
    return pl.pallas_call(
        combine_kernel,
        out_shape=jax.ShapeDtypeStruct((rows, width), jnp.bfloat16),
        in_specs=[vmem] * 6,
        out_specs=vmem,
        compiler_params=small,
        name="combine",
    )(routes.T, gate_scores.T, pick, expert, states, returned)


def solution(mesh):
    cores, chips = mesh.devices.shape
    side = round(chips ** (1 / 3))
    return jax.shard_map(
        body,
        mesh=Mesh(mesh.devices.reshape(cores, side, side, side), axes),
        in_specs=(
            P(axes, None),
            P(axes, None),
            P(axes, None),
            P(axes, None, None),
            P(axes, None, None),
        ),
        out_specs=P(axes, None),
        check_vma=False,
    )
```

```python
import functools

import jax
import jax.numpy as jnp
from jax import lax
from jax.experimental import pallas as pl
from jax.experimental.pallas import tpu as pltpu
from jax.sharding import Mesh
from jax.sharding import PartitionSpec as P

route_scale = 2.5
axes = ("grp", "x", "y", "z")
turn = ("grp", "z", "y", "x")
most = 2


def column_kernel(sizes, expert_ref):
    left = lax.broadcasted_iota(jnp.int32, expert_ref.shape, 0) // most
    place = {}
    for axis in reversed(turn):
        place[axis] = left % sizes[axis]
        left = left // sizes[axis]
    expert = jnp.zeros_like(left)
    for axis in axes:
        expert = expert * sizes[axis] + place[axis]
    expert_ref[...] = expert


def pick_kernel(routes_ref, expert_ref, pick_ref):
    expert = expert_ref[...]
    top, rows = routes_ref.shape
    named = jnp.zeros(expert.shape, jnp.float32)
    for k in range(top):
        named = jnp.where(routes_ref[k : k + 1, :] == expert, 1.0, named)
    earlier = (
        lax.broadcasted_iota(jnp.int32, (rows, rows), 0)
        < lax.broadcasted_iota(jnp.int32, (rows, rows), 1)
    ).astype(jnp.float32)
    position = jnp.dot(
        named.astype(jnp.bfloat16), earlier.astype(jnp.bfloat16), preferred_element_type=jnp.float32
    )
    slot = (lax.broadcasted_iota(jnp.int32, expert.shape, 0) % most).astype(jnp.float32)
    pick_ref[...] = jnp.where(jnp.abs(position - slot) < 0.5, named, 0.0).astype(jnp.bfloat16)


def dispatch_kernel(pick_ref, states_ref, routes_ref, scores_ref, expert_ref, out_ref, mix_ref):
    experts, _, width = out_ref.shape
    pick = pick_ref[...]
    tile = 512
    for c in range(0, width, tile):
        block = jnp.dot(pick, states_ref[:, c : c + tile], preferred_element_type=jnp.float32)
        out_ref[:, :, c : c + tile] = block.astype(jnp.bfloat16).reshape(experts, most, tile)
    scores = scores_ref[...]
    expert = expert_ref[...]
    weights = scores / jnp.sum(scores, axis=0, keepdims=True) * route_scale
    weight = jnp.zeros(expert.shape, jnp.float32)
    for k in range(routes_ref.shape[0]):
        weight = jnp.where(routes_ref[k : k + 1, :] == expert, weights[k : k + 1, :], weight)
    high = weight.astype(jnp.bfloat16)
    low = (weight - high.astype(jnp.float32)).astype(jnp.bfloat16)
    mix_ref[...] = jnp.concatenate([pick * high, pick * low], axis=1)


def ffn_kernel(in_ref, first, second, out_ref, rows_in, hidden):
    inner, width = second.shape[1:]
    rows_in[...] = in_ref[...].reshape(rows_in.shape)
    tile = 256
    for c in range(0, inner, tile):
        gate = jnp.dot(rows_in[...], first[0, :, c : c + tile], preferred_element_type=jnp.float32)
        up = jnp.dot(
            rows_in[...], first[0, :, inner + c : inner + c + tile], preferred_element_type=jnp.float32
        )
        hidden[:, c : c + tile] = (gate / (1.0 + jnp.exp(-gate)) * up).astype(jnp.bfloat16)
    tile = 512
    for c in range(0, width, tile):
        block = jnp.dot(hidden[...], second[0, :, c : c + tile], preferred_element_type=jnp.float32)
        out_ref[:, :, c : c + tile] = block.astype(jnp.bfloat16).reshape(-1, most, tile)


def combine_kernel(mix_ref, states_ref, got_ref, out_hbm, out_ref, sems):
    rows, width = states_ref.shape
    tile = width // 2
    copies = []
    for c in range(0, width, tile):
        here = pl.ds(c, tile)
        got = got_ref[:, :, here].reshape(-1, tile)
        total = lax.dot_general(
            mix_ref[...], got, (((0,), (0,)), ((), ())), preferred_element_type=jnp.float32
        )
        mixed = states_ref[:, here].astype(jnp.float32) + (total[:rows] + total[rows:])
        out_ref[:, here] = mixed.astype(jnp.bfloat16)
        copies.append(pltpu.make_async_copy(out_ref.at[:, here], out_hbm.at[:, here], sems.at[c // tile]))
        copies[-1].start()
    for copy in copies:
        copy.wait()


def body(states, routes, gate_scores, w_in, w_out):
    rows, width = states.shape
    experts = lax.axis_size(axes)
    slots = experts * most
    inner = w_out.shape[1]
    work = 2 * slots * width * inner * 3
    weights = 2 * width * inner * 3
    vmem = pl.BlockSpec(memory_space=pltpu.VMEM)
    message = jax.ShapeDtypeStruct((experts, most, width), jnp.bfloat16)
    small = pltpu.CompilerParams(vmem_limit_bytes=8 << 20)

    expert = pl.pallas_call(
        functools.partial(column_kernel, {axis: lax.axis_size(axis) for axis in axes}),
        out_shape=jax.ShapeDtypeStruct((slots, rows), jnp.int32),
        out_specs=vmem,
        compiler_params=small,
        cost_estimate=pl.CostEstimate(flops=16 * work, bytes_accessed=8 * weights, transcendentals=0),
        name="columns",
    )()
    pick = pl.pallas_call(
        pick_kernel,
        out_shape=jax.ShapeDtypeStruct((slots, rows), jnp.bfloat16),
        in_specs=[vmem] * 2,
        out_specs=vmem,
        compiler_params=small,
        name="pick",
    )(routes.T, expert)
    outgoing, mix = pl.pallas_call(
        dispatch_kernel,
        out_shape=[message, jax.ShapeDtypeStruct((slots, 2 * rows), jnp.bfloat16)],
        in_specs=[vmem] * 5,
        out_specs=[vmem] * 2,
        compiler_params=small,
        name="dispatch",
    )(pick, states, routes.T, gate_scores.T, expert)
    received = lax.all_to_all(outgoing, turn, split_axis=0, concat_axis=0, tiled=True)
    result = pl.pallas_call(
        ffn_kernel,
        out_shape=message,
        in_specs=[vmem] * 3,
        out_specs=vmem,
        scratch_shapes=[
            pltpu.VMEM((slots, width), jnp.bfloat16),
            pltpu.VMEM((slots, inner), jnp.bfloat16),
        ],
        compiler_params=pltpu.CompilerParams(vmem_limit_bytes=16 << 20),
        cost_estimate=pl.CostEstimate(
            flops=work, bytes_accessed=weights, transcendentals=slots * inner
        ),
        name="expert_ffn",
    )(received, w_in, w_out)
    returned = lax.all_to_all(result, turn, split_axis=0, concat_axis=0, tiled=True)
    return pl.pallas_call(
        combine_kernel,
        out_shape=jax.ShapeDtypeStruct((rows, width), jnp.bfloat16),
        in_specs=[vmem] * 3,
        out_specs=pl.BlockSpec(memory_space=pl.ANY),
        scratch_shapes=[pltpu.VMEM((rows, width), jnp.bfloat16), pltpu.SemaphoreType.DMA((2,))],
        compiler_params=small,
        name="combine",
    )(mix, states, returned)


def solution(mesh):
    cores, chips = mesh.devices.shape
    side = round(chips ** (1 / 3))
    return jax.shard_map(
        body,
        mesh=Mesh(mesh.devices.reshape(cores, side, side, side), axes),
        in_specs=(
            P(axes, None),
            P(axes, None),
            P(axes, None),
            P(axes, None, None),
            P(axes, None, None),
        ),
        out_specs=P(axes, None),
        check_vma=False,
    )
```

```python
import functools

import jax
import jax.numpy as jnp
from jax import lax
from jax.experimental import pallas as pl
from jax.experimental.pallas import tpu as pltpu
from jax.sharding import Mesh
from jax.sharding import PartitionSpec as P

route_scale = 2.5
axes = ("grp", "x", "y", "z")
turn = ("grp", "z", "y", "x")
most = 2


def column_kernel(sizes, expert_ref):
    left = lax.broadcasted_iota(jnp.int32, expert_ref.shape, 0) // most
    place = {}
    for axis in reversed(turn):
        place[axis] = left % sizes[axis]
        left = left // sizes[axis]
    expert = jnp.zeros_like(left)
    for axis in axes:
        expert = expert * sizes[axis] + place[axis]
    expert_ref[...] = expert


def pick_kernel(routes_ref, expert_ref, pick_ref):
    expert = expert_ref[...]
    top, rows = routes_ref.shape
    named = jnp.zeros(expert.shape, jnp.float32)
    for k in range(top):
        named = jnp.where(routes_ref[k : k + 1, :] == expert, 1.0, named)
    earlier = (
        lax.broadcasted_iota(jnp.int32, (rows, rows), 0)
        < lax.broadcasted_iota(jnp.int32, (rows, rows), 1)
    ).astype(jnp.float32)
    position = jnp.dot(
        named.astype(jnp.bfloat16), earlier.astype(jnp.bfloat16), preferred_element_type=jnp.float32
    )
    slot = (lax.broadcasted_iota(jnp.int32, expert.shape, 0) % most).astype(jnp.float32)
    pick_ref[...] = jnp.where(jnp.abs(position - slot) < 0.5, named, 0.0).astype(jnp.bfloat16)


def dispatch_kernel(pick_ref, states_ref, routes_ref, scores_ref, expert_ref, out_ref, mix_ref):
    experts, _, width = out_ref.shape
    pick = pick_ref[...]
    scores = scores_ref[...]
    expert = expert_ref[...]
    weights = scores / jnp.sum(scores, axis=0, keepdims=True) * route_scale
    weight = jnp.zeros(expert.shape, jnp.float32)
    for k in range(routes_ref.shape[0]):
        weight = jnp.where(routes_ref[k : k + 1, :] == expert, weights[k : k + 1, :], weight)
    high = weight.astype(jnp.bfloat16)
    low = (weight - high.astype(jnp.float32)).astype(jnp.bfloat16)
    mix_ref[...] = jnp.concatenate([pick * high, pick * low], axis=1)
    tile = 512
    for c in range(0, width, tile):
        block = jnp.dot(pick, states_ref[:, c : c + tile], preferred_element_type=jnp.float32)
        out_ref[:, :, c : c + tile] = block.astype(jnp.bfloat16).reshape(experts, most, tile)


def ffn_kernel(in_ref, first, second, out_ref, rows_in, hidden):
    inner, width = second.shape[1:]
    rows_in[...] = in_ref[...].reshape(rows_in.shape)
    tile = 256
    for c in range(0, inner, tile):
        gate = jnp.dot(rows_in[...], first[0, :, c : c + tile], preferred_element_type=jnp.float32)
        up = jnp.dot(
            rows_in[...], first[0, :, inner + c : inner + c + tile], preferred_element_type=jnp.float32
        )
        hidden[:, c : c + tile] = (gate / (1.0 + jnp.exp(-gate)) * up).astype(jnp.bfloat16)
    tile = 512
    for c in range(0, width, tile):
        block = jnp.dot(hidden[...], second[0, :, c : c + tile], preferred_element_type=jnp.float32)
        out_ref[:, :, c : c + tile] = block.astype(jnp.bfloat16).reshape(-1, most, tile)


def combine_kernel(mix_ref, states_ref, got_ref, out_hbm, out_ref, sems):
    rows, width = states_ref.shape
    tile = width // 4
    copies = []
    for c in range(0, width, tile):
        here = pl.ds(c, tile)
        got = got_ref[:, :, here].reshape(-1, tile)
        total = lax.dot_general(
            mix_ref[...], got, (((0,), (0,)), ((), ())), preferred_element_type=jnp.float32
        )
        mixed = states_ref[:, here].astype(jnp.float32) + (total[:rows] + total[rows:])
        out_ref[:, here] = mixed.astype(jnp.bfloat16)
        copies.append(pltpu.make_async_copy(out_ref.at[:, here], out_hbm.at[:, here], sems.at[c // tile]))
        copies[-1].start()
    for copy in copies:
        copy.wait()


def body(states, routes, gate_scores, w_in, w_out):
    rows, width = states.shape
    experts = lax.axis_size(axes)
    slots = experts * most
    inner = w_out.shape[1]
    work = 2 * slots * width * inner * 3
    weights = 2 * width * inner * 3
    vmem = pl.BlockSpec(memory_space=pltpu.VMEM)
    message = jax.ShapeDtypeStruct((experts, most, width), jnp.bfloat16)
    small = pltpu.CompilerParams(vmem_limit_bytes=8 << 20)

    expert = pl.pallas_call(
        functools.partial(column_kernel, {axis: lax.axis_size(axis) for axis in axes}),
        out_shape=jax.ShapeDtypeStruct((slots, rows), jnp.int32),
        out_specs=vmem,
        compiler_params=small,
        cost_estimate=pl.CostEstimate(flops=16 * work, bytes_accessed=8 * weights, transcendentals=0),
        name="columns",
    )()
    pick = pl.pallas_call(
        pick_kernel,
        out_shape=jax.ShapeDtypeStruct((slots, rows), jnp.bfloat16),
        in_specs=[vmem] * 2,
        out_specs=vmem,
        compiler_params=small,
        name="pick",
    )(routes.T, expert)
    outgoing, mix = pl.pallas_call(
        dispatch_kernel,
        out_shape=[message, jax.ShapeDtypeStruct((slots, 2 * rows), jnp.bfloat16)],
        in_specs=[vmem] * 5,
        out_specs=[vmem] * 2,
        compiler_params=small,
        name="dispatch",
    )(pick, states, routes.T, gate_scores.T, expert)
    received = lax.all_to_all(outgoing, turn, split_axis=0, concat_axis=0, tiled=True)
    result = pl.pallas_call(
        ffn_kernel,
        out_shape=message,
        in_specs=[vmem] * 3,
        out_specs=vmem,
        scratch_shapes=[
            pltpu.VMEM((slots, width), jnp.bfloat16),
            pltpu.VMEM((slots, inner), jnp.bfloat16),
        ],
        compiler_params=pltpu.CompilerParams(vmem_limit_bytes=16 << 20),
        cost_estimate=pl.CostEstimate(
            flops=work, bytes_accessed=weights, transcendentals=slots * inner
        ),
        name="expert_ffn",
    )(received, w_in, w_out)
    returned = lax.all_to_all(result, turn, split_axis=0, concat_axis=0, tiled=True)
    return pl.pallas_call(
        combine_kernel,
        out_shape=jax.ShapeDtypeStruct((rows, width), jnp.bfloat16),
        in_specs=[vmem] * 3,
        out_specs=pl.BlockSpec(memory_space=pl.ANY),
        scratch_shapes=[pltpu.VMEM((rows, width), jnp.bfloat16), pltpu.SemaphoreType.DMA((4,))],
        compiler_params=small,
        name="combine",
    )(mix, states, returned)


def solution(mesh):
    cores, chips = mesh.devices.shape
    side = round(chips ** (1 / 3))
    return jax.shard_map(
        body,
        mesh=Mesh(mesh.devices.reshape(cores, side, side, side), axes),
        in_specs=(
            P(axes, None),
            P(axes, None),
            P(axes, None),
            P(axes, None, None),
            P(axes, None, None),
        ),
        out_specs=P(axes, None),
        check_vma=False,
    )
```

```python
import functools

import jax
import jax.numpy as jnp
from jax import lax
from jax.experimental import pallas as pl
from jax.experimental.pallas import tpu as pltpu
from jax.sharding import Mesh
from jax.sharding import PartitionSpec as P

route_scale = 2.5
axes = ("grp", "x", "y", "z")
turn = ("grp", "z", "y", "x")
most = 2


def column_kernel(sizes, expert_ref):
    left = lax.broadcasted_iota(jnp.int32, expert_ref.shape, 0) // most
    place = {}
    for axis in reversed(turn):
        place[axis] = left % sizes[axis]
        left = left // sizes[axis]
    expert = jnp.zeros_like(left)
    for axis in axes:
        expert = expert * sizes[axis] + place[axis]
    expert_ref[...] = expert


def pick_kernel(routes_ref, expert_ref, pick_ref):
    expert = expert_ref[...]
    top, rows = routes_ref.shape
    named = jnp.zeros(expert.shape, jnp.float32)
    for k in range(top):
        named = jnp.where(routes_ref[k : k + 1, :] == expert, 1.0, named)
    earlier = (
        lax.broadcasted_iota(jnp.int32, (rows, rows), 0)
        < lax.broadcasted_iota(jnp.int32, (rows, rows), 1)
    ).astype(jnp.float32)
    position = jnp.dot(
        named.astype(jnp.bfloat16), earlier.astype(jnp.bfloat16), preferred_element_type=jnp.float32
    )
    slot = (lax.broadcasted_iota(jnp.int32, expert.shape, 0) % most).astype(jnp.float32)
    pick_ref[...] = jnp.where(jnp.abs(position - slot) < 0.5, named, 0.0).astype(jnp.bfloat16)


def dispatch_kernel(pick_ref, states_ref, routes_ref, scores_ref, expert_ref, out_ref, mix_ref):
    experts, _, width = out_ref.shape
    pick = pick_ref[...]
    scores = scores_ref[...]
    expert = expert_ref[...]
    weights = scores / jnp.sum(scores, axis=0, keepdims=True) * route_scale
    weight = jnp.zeros(expert.shape, jnp.float32)
    for k in range(routes_ref.shape[0]):
        weight = jnp.where(routes_ref[k : k + 1, :] == expert, weights[k : k + 1, :], weight)
    high = weight.astype(jnp.bfloat16)
    low = (weight - high.astype(jnp.float32)).astype(jnp.bfloat16)
    mix_ref[...] = jnp.concatenate([pick * high, pick * low], axis=1)
    tile = width // 2
    for c in range(0, width, tile):
        block = jnp.dot(pick, states_ref[:, c : c + tile], preferred_element_type=jnp.float32)
        out_ref[:, :, c : c + tile] = block.astype(jnp.bfloat16).reshape(experts, most, tile)


def ffn_kernel(in_ref, first, second, out_ref, rows_in, hidden):
    inner, width = second.shape[1:]
    rows_in[...] = in_ref[...].reshape(rows_in.shape)
    tile = 256
    for c in range(0, inner, tile):
        gate = jnp.dot(rows_in[...], first[0, :, c : c + tile], preferred_element_type=jnp.float32)
        up = jnp.dot(
            rows_in[...], first[0, :, inner + c : inner + c + tile], preferred_element_type=jnp.float32
        )
        hidden[:, c : c + tile] = (gate / (1.0 + jnp.exp(-gate)) * up).astype(jnp.bfloat16)
    tile = 512
    for c in range(0, width, tile):
        block = jnp.dot(hidden[...], second[0, :, c : c + tile], preferred_element_type=jnp.float32)
        out_ref[:, :, c : c + tile] = block.astype(jnp.bfloat16).reshape(-1, most, tile)


def combine_kernel(mix_ref, states_ref, got_ref, out_hbm, out_ref, sems):
    rows, width = states_ref.shape
    tile = width // 4
    copies = []
    for c in range(0, width, tile):
        here = pl.ds(c, tile)
        got = got_ref[:, :, here].reshape(-1, tile)
        total = lax.dot_general(
            mix_ref[...], got, (((0,), (0,)), ((), ())), preferred_element_type=jnp.float32
        )
        mixed = states_ref[:, here].astype(jnp.float32) + (total[:rows] + total[rows:])
        out_ref[:, here] = mixed.astype(jnp.bfloat16)
        copies.append(pltpu.make_async_copy(out_ref.at[:, here], out_hbm.at[:, here], sems.at[c // tile]))
        copies[-1].start()
    for copy in copies:
        copy.wait()


def body(states, routes, gate_scores, w_in, w_out):
    rows, width = states.shape
    experts = lax.axis_size(axes)
    slots = experts * most
    inner = w_out.shape[1]
    work = 2 * slots * width * inner * 3
    weights = 2 * width * inner * 3
    vmem = pl.BlockSpec(memory_space=pltpu.VMEM)
    message = jax.ShapeDtypeStruct((experts, most, width), jnp.bfloat16)
    small = pltpu.CompilerParams(vmem_limit_bytes=8 << 20)

    expert = pl.pallas_call(
        functools.partial(column_kernel, {axis: lax.axis_size(axis) for axis in axes}),
        out_shape=jax.ShapeDtypeStruct((slots, rows), jnp.int32),
        out_specs=vmem,
        compiler_params=small,
        cost_estimate=pl.CostEstimate(flops=16 * work, bytes_accessed=8 * weights, transcendentals=0),
        name="columns",
    )()
    pick = pl.pallas_call(
        pick_kernel,
        out_shape=jax.ShapeDtypeStruct((slots, rows), jnp.bfloat16),
        in_specs=[vmem] * 2,
        out_specs=vmem,
        compiler_params=small,
        name="pick",
    )(routes.T, expert)
    outgoing, mix = pl.pallas_call(
        dispatch_kernel,
        out_shape=[message, jax.ShapeDtypeStruct((slots, 2 * rows), jnp.bfloat16)],
        in_specs=[vmem] * 5,
        out_specs=[vmem] * 2,
        compiler_params=small,
        name="dispatch",
    )(pick, states, routes.T, gate_scores.T, expert)
    received = lax.all_to_all(outgoing, turn, split_axis=0, concat_axis=0, tiled=True)
    result = pl.pallas_call(
        ffn_kernel,
        out_shape=message,
        in_specs=[vmem] * 3,
        out_specs=vmem,
        scratch_shapes=[
            pltpu.VMEM((slots, width), jnp.bfloat16),
            pltpu.VMEM((slots, inner), jnp.bfloat16),
        ],
        compiler_params=pltpu.CompilerParams(vmem_limit_bytes=16 << 20),
        cost_estimate=pl.CostEstimate(
            flops=work, bytes_accessed=weights, transcendentals=slots * inner
        ),
        name="expert_ffn",
    )(received, w_in, w_out)
    returned = lax.all_to_all(result, turn, split_axis=0, concat_axis=0, tiled=True)
    return pl.pallas_call(
        combine_kernel,
        out_shape=jax.ShapeDtypeStruct((rows, width), jnp.bfloat16),
        in_specs=[vmem] * 3,
        out_specs=pl.BlockSpec(memory_space=pl.ANY),
        scratch_shapes=[pltpu.VMEM((rows, width), jnp.bfloat16), pltpu.SemaphoreType.DMA((4,))],
        compiler_params=small,
        name="combine",
    )(mix, states, returned)


def solution(mesh):
    cores, chips = mesh.devices.shape
    side = round(chips ** (1 / 3))
    return jax.shard_map(
        body,
        mesh=Mesh(mesh.devices.reshape(cores, side, side, side), axes),
        in_specs=(
            P(axes, None),
            P(axes, None),
            P(axes, None),
            P(axes, None, None),
            P(axes, None, None),
        ),
        out_specs=P(axes, None),
        check_vma=False,
    )
```
